32 devices in a mesh: rep: 2 (over y), grp: 4 (over z), sub: 4 (over x, core).
Axes of the slice: x: 2, y: 2, z: 4, core: 2. Of those that a mesh axis runs over, the one named last changes fastest.
Arguments:
- embeddings: bfloat16 [8192, 1024], P(('rep', 'grp', 'sub')), parts along dimension 0, may hold values from -6 to 6
- cluster_ids: int32 [8192, 1], P(('rep', 'grp', 'sub')), parts along dimension 0, may hold values from 0 to 3; in each aligned block of 256 rows (0 to 255, 256 to 511, ...) at most 128 rows name the same one
Outputs:
- max_similarity: float32 [8192], P(('rep', 'grp', 'sub')), parts along dimension 0
The draws below stay inside these ranges and needn't reach their ends.
There are 2 independent parts, one for each index of `rep`. The reference program is written for one: setup_inputs(seed, part) draws one part's arguments, and reference() takes and returns one part's arrays. A program takes and returns all parts, laid end to end along the dimension named above; each array names one. Nothing has to cross between parts.
Inputs may be any that keep to these rules, and one draw needn't show every extreme that they name: `cluster_ids`: cluster numbers run from 0 to 3; among the rows of one device no cluster is named by more than 128 rows, and in every draw some cluster is named by exactly 128 rows of some device.
All inputs are finite; a program needn't handle non-finite values.
Results may differ from the reference program's by a relative error of at most 0.0014.
Values may be sent and summed in bfloat16 or wider, within the bound.
No kernel may reach another device: no remote copies, remote signals or barrier semaphores. Data moves between devices by JAX's collectives and lax.ppermute only.
A program may use at most 64 MiB of HBM per device.

```python
import math
import jax
import jax.numpy as jnp
import numpy as np
from jax import lax

D = 1024
ROWS_DEV = 256
CAP = 128
CLUSTERS = 4
DOCS = 4096
N_GRP = 4
N_SUB = 4


def shard_levels(key, shape, pieces, smallest, top_value):
    loudness = 1.0
    for axis_at, blocks in pieces:
        heights = jax.random.uniform(jax.random.fold_in(jax.random.fold_in(key, 6), axis_at), (blocks,), jnp.float32, smallest / len(pieces), top_value / len(pieces))
        loudness = loudness * jnp.repeat(jnp.exp(heights), shape[axis_at] // blocks).reshape((-1,) + (1,) * (len(shape) - 1 - axis_at))
    return loudness


def shared_out(key, own, number, rows, number_of, top, reach, lean):
    sequence = jax.random.permutation(key, number_of)
    crowded, common = load_shares(number_of, rows * top, reach, lean, True), load_shares(number_of, rows * top, reach, lean, False)
    places = jnp.arange(number_of)

    def named(sizes, turn):
        used = int((sizes > 0).sum())
        fixed = max(1, used // 4)
        passed = fixed + (places - fixed + turn * (used - fixed)) % max(1, number_of - fixed)
        return jnp.zeros((number_of,), jnp.int32).at[sequence[jnp.where(places < fixed, places, passed)]].set(jnp.asarray(sizes, jnp.int32))

    sizes = jnp.where(number % 4 == 0, named(crowded, number // 4), named(common, number - number // 4 - 1))
    mixed = jax.random.permutation(jax.random.fold_in(own, 3), number_of)
    source_of, sink = mixed[0:number_of // 2 * 2:2], mixed[1:number_of // 2 * 2:2]
    slack = jnp.minimum(sizes[source_of] - 1, reach - sizes[sink]) // 2
    slack = jnp.where((source_of == sequence[0]) | (sink == sequence[0]) | (sizes[sink] == 0), 0, jnp.maximum(slack, 0))
    passed = jax.random.randint(jax.random.fold_in(own, 4), (number_of // 2,), 0, 1 << 20) % (slack + 1)
    sizes = sizes.at[source_of].add(-passed).at[sink].add(passed)
    items = jnp.searchsorted(jnp.cumsum(sizes), jnp.arange(rows * top), side="right").astype(jnp.int32)
    table = items.reshape(top, rows).T
    table = table[jax.random.permutation(jax.random.fold_in(own, 1), rows)]
    turn = jax.random.randint(jax.random.fold_in(own, 2), (rows, 1), 0, top)
    return jnp.take_along_axis(table, (jnp.arange(top)[None, :] + turn) % top, axis=1)


def load_shares(number_of, total, limit, skew, full):
    portions = [(1 << 20) // math.isqrt(grade ** skew) + 1 for grade in range(1, number_of + 1)]
    largest = limit if full else min(limit, max(-(-total // number_of), total * portions[0] // sum(portions)))
    least = 1 if total - largest >= number_of - 1 else 0
    given, surplus = [largest] + [least] * (number_of - 1), total - largest - least * (number_of - 1)
    while surplus > 0:
        candidates = [i for i in range(1, number_of) if given[i] < largest] or [i for i in range(1, number_of) if given[i] < limit]
        mass, remaining = sum([portions[i] for i in candidates]), surplus
        for i in candidates:
            more = min(limit - given[i], max(1, remaining * portions[i] // mass), surplus)
            given[i] = given[i] + more
            surplus = surplus - more
    return np.array(given)


def centred(own_key, dims, width, reach, split=(), kind=jnp.bfloat16):
    loudness = shard_levels(own_key, dims, split, -0.22, 0.18) if split else 1.0
    result = jax.random.normal(own_key, dims, jnp.float32) * width * loudness
    return jnp.minimum(jnp.maximum(result, -reach), reach).astype(kind)


def setup_inputs(seed: int = 0, part: int = 0) -> dict:
    key_list = jax.random.split(jax.random.key(seed), 3)
    part_splits = jax.random.split(jax.random.fold_in(key_list[2], part), 3)
    embeddings = centred(part_splits[0], (DOCS, D), 1.0, 6.0, ((0, 16),))
    cluster_ids_keys = jax.random.split(jax.random.fold_in(part_splits[1], 1), DOCS // ROWS_DEV)
    cluster_ids_turns = jax.random.permutation(jax.random.fold_in(part_splits[1], 3), DOCS // ROWS_DEV)
    cluster_ids = jax.vmap(lambda own, number: shared_out(jax.random.fold_in(part_splits[1], 2), own, number, ROWS_DEV, CLUSTERS, 1, CAP, 2))(cluster_ids_keys, cluster_ids_turns).reshape((DOCS, 1))
    return dict(embeddings=embeddings, cluster_ids=cluster_ids)


def reference(embeddings, cluster_ids):
    floats = embeddings.astype(jnp.float32)
    unit_rows = (floats * lax.rsqrt(lax.optimization_barrier(jnp.mean(floats * floats, axis=1, keepdims=True)) + 1e-06) / math.sqrt(D)).astype(jnp.bfloat16)
    labels = cluster_ids[:, 0].astype(jnp.int32)
    doc_total = labels.shape[0]
    ordering = jnp.argsort(labels, stable=True).astype(jnp.int32)
    sorted_labels = labels[ordering]
    tallies = jax.ops.segment_sum(jnp.ones_like(labels), labels, CLUSTERS).astype(jnp.int32)
    offsets = (jnp.cumsum(tallies) - tallies).astype(jnp.int32)
    within = (jnp.arange(doc_total, dtype=jnp.int32) - offsets[sorted_labels]).astype(jnp.int32)
    longest = CAP * N_GRP * N_SUB
    packed = jnp.zeros((CLUSTERS, longest, D), embeddings.dtype).at[sorted_labels, within].set(unit_rows[ordering])
    occupied = jnp.zeros((CLUSTERS, longest), jnp.int32).at[sorted_labels, within].set(1)
    diagonal_mask = jnp.eye(longest, dtype=bool)

    def cluster_maxima(pair):
        members, present = pair
        values = members.astype(jnp.float32)
        similar = jnp.dot(values, values.T, precision=lax.Precision.HIGHEST, preferred_element_type=jnp.float32)
        allowed = (present[None, :] > 0) & jnp.logical_not(diagonal_mask)
        return lax.optimization_barrier(jnp.max(jnp.where(allowed, similar, jnp.float32(-1.0)), axis=1))
    highest = lax.map(cluster_maxima, (packed, occupied))
    picked = highest[sorted_labels, within]
    return jnp.zeros((doc_total,), jnp.float32).at[ordering].set(picked)
```

```python
import functools
import math

import jax
import jax.numpy as jnp
from jax import lax
from jax.experimental import pallas as pl
from jax.experimental.pallas import tpu as pltpu
from jax.sharding import PartitionSpec as P

PIECES = 8
VMEM = pl.BlockSpec(memory_space=pltpu.VMEM)
SMEM = pl.BlockSpec(memory_space=pltpu.SMEM)


def from_behind(value, axis, by):
    peers = lax.axis_size(axis)
    return lax.ppermute(value, axis, [(i, (i + by) % peers) for i in range(peers)])


def masked_maxima(left_rows, right_rows, right_present, excluded):
    similar = jnp.dot(left_rows, right_rows.T, preferred_element_type=jnp.float32)
    allowed = (right_present[None, :] > 0) & jnp.logical_not(excluded)
    return jnp.where(allowed, similar, jnp.float32(-1.0))


def clustered(embeddings, cluster_ids):
    rows_dev, features = embeddings.shape
    groups = lax.axis_size("grp")
    subgroup = lax.axis_size("sub")
    capacity = 2 * rows_dev // groups
    unit_rows = unit(embeddings)
    labels = cluster_ids[:, 0]
    member_table = (labels[:, None] == jnp.arange(groups, dtype=jnp.int32)[None, :]).astype(
        jnp.int32
    )
    running = jnp.cumsum(member_table, axis=0)
    within = jnp.sum(jnp.where(member_table > 0, running - 1, 0), axis=1)
    slot_index = labels * capacity + within
    outgoing = jnp.zeros((groups * capacity, features), jnp.bfloat16).at[slot_index].set(unit_rows)
    occupied = jnp.zeros((groups * capacity,), jnp.int32).at[slot_index].set(1)
    arrived, arrived_present = (
        lax.all_to_all(
            outgoing.reshape(groups, capacity, features),
            "grp",
            split_axis=0,
            concat_axis=0,
            tiled=True,
        ),
        lax.all_to_all(
            occupied.reshape(groups, capacity), "grp", split_axis=0, concat_axis=0, tiled=True
        ),
    )
    owned_rows = arrived.reshape(groups * capacity, features)
    present = arrived_present.reshape(groups * capacity)
    held = owned_rows.shape[0]
    positions = jnp.arange(held, dtype=jnp.int32)
    excluded = positions[:, None] == positions[None, :]
    highest = jnp.max(masked_maxima(owned_rows, owned_rows, present, excluded), axis=1)
    no_exclusion = jnp.zeros((held, held), dtype=bool)
    for offset in range(1, subgroup // 2 + 1):
        peer_rows, peer_present = from_behind((owned_rows, present), "sub", offset)
        scores = masked_maxima(owned_rows, peer_rows, peer_present, no_exclusion)
        highest = jnp.maximum(highest, jnp.max(scores, axis=1))
        if 2 * offset != subgroup:
            column_best = jnp.max(
                jnp.where(present[:, None] > 0, scores, jnp.float32(-1.0)), axis=0
            )
            returned_best = from_behind(column_best, "sub", -offset)
            highest = jnp.maximum(highest, returned_best)
    returned = lax.all_to_all(
        highest.reshape(groups, capacity), "grp", split_axis=0, concat_axis=0, tiled=True
    )
    return returned.reshape(groups * capacity)[slot_index]


def unit(rows):
    floats = rows.astype(jnp.float32)
    square = jnp.mean(floats * floats, axis=1, keepdims=True)
    return (floats * lax.rsqrt(square + 1e-06) / math.sqrt(rows.shape[1])).astype(jnp.bfloat16)


def own_kernel(rows_hbm, names_hbm, own_ref, rows_ref, names_ref, arrived):
    size = rows_ref.shape[0]
    pieces = arrived.shape[0] - 1
    step = size // pieces
    copies = [
        pltpu.make_async_copy(
            rows_hbm.at[pl.ds(at * step, step)], rows_ref.at[pl.ds(at * step, step)], arrived.at[at]
        )
        for at in range(pieces)
    ]
    copies.append(pltpu.make_async_copy(names_hbm, names_ref, arrived.at[pieces]))
    for copy in copies:
        copy.start()
    for at in range(pieces):
        copies[at].wait()
        own_ref[at * step : (at + 1) * step] = unit(rows_ref[at * step : (at + 1) * step])
    copies[pieces].wait()
    names = names_ref[...].astype(jnp.float32).astype(jnp.bfloat16)
    names = jnp.concatenate(
        [names, jnp.zeros((1, own_ref.shape[1] - size), jnp.bfloat16)], axis=1
    )
    own_ref[size:] = jnp.broadcast_to(names, (own_ref.shape[0] - size, names.shape[1]))


def labels_in(ref, size):
    below = size if ref.shape[0] > size else size // 2
    return ref[below:][:1, :size].astype(jnp.float32)


def best_of(columns, row_labels, names, rows, skip_own=False):
    step = columns.shape[0]
    scores = lax.dot_general(
        columns, rows, (((1,), (1,)), ((), ())), preferred_element_type=jnp.float32
    )
    tall = jnp.broadcast_to(names, (128, step)).T
    tall = jnp.concatenate([tall] * (rows.shape[0] // 128), axis=1)
    allowed = tall == row_labels
    if skip_own:
        down = lax.broadcasted_iota(jnp.int32, scores.shape, 0)
        across = lax.broadcasted_iota(jnp.int32, scores.shape, 1)
        allowed = allowed & (down != across)
    return jnp.max(jnp.where(allowed, scores, -1.0), axis=0, keepdims=True)


def pair_kernel(own_ref, core_ref, best_ref):
    size = best_ref.shape[1]
    own, labels = own_ref[:size], labels_in(own_ref, size)
    best = jnp.maximum(best_of(own, labels, labels, own, True), -1.0)
    found = best_of(core_ref[:size], labels, labels_in(core_ref, size), own)
    best_ref[...] = jnp.maximum(best, found)


def halves_kernel(first_ref, second_ref, upper_ref, lower_ref, across_ref):
    half = lower_ref.shape[0]
    upper_ref[:half] = first_ref[:half]
    upper_ref[half:] = first_ref[2 * half :]
    lower_ref[...] = second_ref[half : 2 * half]
    across_ref[:half] = second_ref[:half]
    across_ref[half:] = second_ref[2 * half :]


def columns_in(refs, size):
    refs, found = list(refs), []
    while refs:
        first = refs.pop(0)
        if first.shape[0] > size:
            found.append((first[:size], labels_in(first, size)))
        else:
            columns = jnp.concatenate([first[: size // 2], refs.pop(0)[...]], axis=0)
            found.append((columns, labels_in(first, size)))
    return found


def best_over(refs, rows, row_labels, size, best):
    for columns, names in columns_in(refs, size):
        best = jnp.maximum(best, best_of(columns, row_labels, names, rows))
    return best


def place_kernel(own_ref, core_ref, before_ref, peer_ref, *refs):
    rows_ref, row_labels_ref, best_ref = refs[-3:]
    size = before_ref.shape[1]
    peer_labels = labels_in(peer_ref, size)
    rows_ref[:size] = own_ref[:size]
    rows_ref[size:] = peer_ref[:size]
    row_labels_ref[:, :size] = labels_in(own_ref, size)
    row_labels_ref[:, size:] = peer_labels
    peer_best = jnp.full((1, size), -1.0, jnp.float32)
    peer_best = best_over((own_ref, core_ref), peer_ref[:size], peer_labels, size, peer_best)
    best = jnp.concatenate([before_ref[...], peer_best], axis=1)
    best_ref[...] = best_over(refs[:-3], rows_ref[...], row_labels_ref[...], size, best)


def near_kernel(rows_ref, row_labels_ref, before_ref, *refs):
    size = row_labels_ref.shape[1] // 2
    refs[-1][...] = best_over(
        refs[:-1], rows_ref[...], row_labels_ref[...], size, before_ref[...]
    )


def half_of(ref, upper_ref, size):
    half = size // 2
    names = labels_in(upper_ref, size)
    return ref[:half], names[:, :half] if ref is upper_ref else names[:, half:]


def far_kernel(far_ref, *refs):
    last_ref, best_ref = refs[-2:]
    size = best_ref.shape[1]
    rows, row_labels = far_ref[:size], labels_in(far_ref, size)
    best = jnp.full(best_ref.shape, -1.0, jnp.float32)
    best = best_over(refs[:-2], rows, row_labels, size, best)
    columns, names = half_of(last_ref, last_ref, size)
    best_ref[...] = jnp.maximum(best, best_of(columns, row_labels, names, rows))


def end_kernel(far_ref, upper_ref, lower_ref, before_ref, best_ref):
    size = best_ref.shape[1]
    columns, names = half_of(lower_ref, upper_ref, size)
    found = best_of(columns, labels_in(far_ref, size), names, far_ref[:size])
    best_ref[...] = jnp.maximum(before_ref[...], found)


def rows_kernel(rows_ref, row_labels_ref, before_ref, *refs):
    own_ref, peer_ref = refs[-2:]
    size = own_ref.shape[1]
    best = best_over(refs[:-2], rows_ref[...], row_labels_ref[...], size, before_ref[...])
    own_ref[...] = best[:, :size]
    peer_ref[...] = best[:, size:]


def larger_kernel(first_ref, second_ref, best_ref):
    best_ref[...] = jnp.maximum(first_ref[...], second_ref[...])


def call(kernel, outs, args, name, flops=1, **more):
    more.setdefault("in_specs", [VMEM] * len(args))
    return pl.pallas_call(
        kernel,
        out_shape=outs,
        out_specs=jax.tree.map(lambda _: VMEM, outs),
        compiler_params=pltpu.CompilerParams(vmem_limit_bytes=32 * 2**20),
        cost_estimate=flops and pl.CostEstimate(flops=flops, bytes_accessed=0, transcendentals=0),
        name=name,
        **more,
    )(*args)


def after(value, *others):
    return lax.optimization_barrier((value,) + others)[0]


def dense(embeddings, cluster_ids):
    rows_dev, features = embeddings.shape
    groups, subgroup = lax.axis_size("grp"), lax.axis_size("sub")
    half = rows_dev // 2
    bf16 = functools.partial(jax.ShapeDtypeStruct, dtype=jnp.bfloat16)
    f32 = functools.partial(jax.ShapeDtypeStruct, dtype=jnp.float32)
    inner = groups // 2

    def core(v):
        return lax.ppermute(v, "sub", [(s, s ^ 1) for s in range(subgroup)])

    def cross(v):
        return lax.ppermute(v, "sub", [(s, s ^ 2) for s in range(subgroup)])

    def beside(v):
        return lax.ppermute(v, "grp", [(g, g ^ 1) for g in range(groups)])

    def middle(v):
        pairs = []
        for g in range(groups):
            for s in range(subgroup):
                other = (groups - 1 - g, s) if g in (inner - 1, inner) else (g, s ^ 1)
                pairs.append((g * subgroup + s, other[0] * subgroup + other[1]))
        return lax.ppermute(v, ("grp", "sub"), pairs)

    def skip_one(v):
        return lax.ppermute(v, "grp", [(g, (g + inner) % groups) for g in range(groups)])

    extra = 8
    own = call(
        own_kernel,
        bf16((rows_dev + extra, features)),
        [
            pltpu.with_memory_space_constraint(v, pltpu.HBM)
            for v in (embeddings, cluster_ids[:, 0][None, :])
        ],
        "own_rows",
        in_specs=[pl.BlockSpec(memory_space=pltpu.HBM)] * 2,
        scratch_shapes=[
            pltpu.VMEM((rows_dev, features), embeddings.dtype),
            pltpu.VMEM((1, rows_dev), cluster_ids.dtype),
            pltpu.SemaphoreType.DMA((PIECES + 1,)),
        ],
    )
    near, peer, across, pair = beside(own), middle(own), cross(own), core(own)
    mine = call(pair_kernel, f32((1, rows_dev)), (own, pair), "own_pair")
    far = middle(near)
    near_upper, across_lower, across_upper = call(
        halves_kernel,
        (
            bf16((half + extra, features)),
            bf16((half, features)),
            bf16((half + extra, features)),
        ),
        (after(near, peer), across),
        "halves",
    )
    across_pair = [core(after(across_upper, mine)), core(across_lower)]
    near_pair = core(near)
    upper, lower = cross(near_upper), beside(across_lower)
    rows, row_labels, best = call(
        place_kernel,
        (bf16((2 * rows_dev, features)), f32((1, 2 * rows_dev)), f32((1, 2 * rows_dev))),
        [own, pair, mine, peer, across] + across_pair,
        "own_place",
    )
    best = call(
        near_kernel,
        f32((1, 2 * rows_dev)),
        (rows, row_labels, best, near, near_pair),
        "beside",
    )
    upper_pair = core(after(upper, best))
    lower_pair = core(after(lower, far))
    for_far = call(
        far_kernel,
        f32((1, rows_dev)),
        [far, own, pair, across] + across_pair + [near, near_pair, upper, lower, upper_pair],
        "far_rows",
    )
    for_far = call(
        end_kernel, f32((1, rows_dev)), (far, upper_pair, lower_pair, for_far), "far_rows_end"
    )
    from_far = skip_one(for_far)
    mine, for_peer = call(
        rows_kernel,
        (f32((1, rows_dev)),) * 2,
        (rows, row_labels, best, upper, lower, upper_pair, lower_pair),
        "beside_other",
    )
    from_peer = middle(for_peer)
    with_far = call(larger_kernel, f32((1, rows_dev)), (mine, from_far), "larger")
    place = lax.axis_index("grp")
    is_inner = (place == inner - 1) | (place == inner)
    return jnp.where(is_inner, jnp.maximum(mine, from_peer), with_far)[0]


def solution(mesh):
    fits = mesh.shape["grp"] == mesh.shape["sub"] == 2 * 2
    return jax.shard_map(
        dense if fits else clustered,
        mesh=mesh,
        in_specs=(P(("rep", "grp", "sub"), None), P(("rep", "grp", "sub"), None)),
        out_specs=P(("rep", "grp", "sub")),
        check_vma=False,
    )
```

```python
import functools
import math

import jax
import jax.numpy as jnp
from jax import lax
from jax.experimental import pallas as pl
from jax.experimental.pallas import tpu as pltpu
from jax.sharding import PartitionSpec as P

PIECES = 2
VMEM = pl.BlockSpec(memory_space=pltpu.VMEM)
SMEM = pl.BlockSpec(memory_space=pltpu.SMEM)


def from_behind(value, axis, by):
    peers = lax.axis_size(axis)
    return lax.ppermute(value, axis, [(i, (i + by) % peers) for i in range(peers)])


def masked_maxima(left_rows, right_rows, right_present, excluded):
    similar = jnp.dot(left_rows, right_rows.T, preferred_element_type=jnp.float32)
    allowed = (right_present[None, :] > 0) & jnp.logical_not(excluded)
    return jnp.where(allowed, similar, jnp.float32(-1.0))


def clustered(embeddings, cluster_ids):
    rows_dev, features = embeddings.shape
    groups = lax.axis_size("grp")
    subgroup = lax.axis_size("sub")
    capacity = 2 * rows_dev // groups
    unit_rows = unit(embeddings)
    labels = cluster_ids[:, 0]
    member_table = (labels[:, None] == jnp.arange(groups, dtype=jnp.int32)[None, :]).astype(
        jnp.int32
    )
    running = jnp.cumsum(member_table, axis=0)
    within = jnp.sum(jnp.where(member_table > 0, running - 1, 0), axis=1)
    slot_index = labels * capacity + within
    outgoing = jnp.zeros((groups * capacity, features), jnp.bfloat16).at[slot_index].set(unit_rows)
    occupied = jnp.zeros((groups * capacity,), jnp.int32).at[slot_index].set(1)
    arrived, arrived_present = (
        lax.all_to_all(
            outgoing.reshape(groups, capacity, features),
            "grp",
            split_axis=0,
            concat_axis=0,
            tiled=True,
        ),
        lax.all_to_all(
            occupied.reshape(groups, capacity), "grp", split_axis=0, concat_axis=0, tiled=True
        ),
    )
    owned_rows = arrived.reshape(groups * capacity, features)
    present = arrived_present.reshape(groups * capacity)
    held = owned_rows.shape[0]
    positions = jnp.arange(held, dtype=jnp.int32)
    excluded = positions[:, None] == positions[None, :]
    highest = jnp.max(masked_maxima(owned_rows, owned_rows, present, excluded), axis=1)
    no_exclusion = jnp.zeros((held, held), dtype=bool)
    for offset in range(1, subgroup // 2 + 1):
        peer_rows, peer_present = from_behind((owned_rows, present), "sub", offset)
        scores = masked_maxima(owned_rows, peer_rows, peer_present, no_exclusion)
        highest = jnp.maximum(highest, jnp.max(scores, axis=1))
        if 2 * offset != subgroup:
            column_best = jnp.max(
                jnp.where(present[:, None] > 0, scores, jnp.float32(-1.0)), axis=0
            )
            returned_best = from_behind(column_best, "sub", -offset)
            highest = jnp.maximum(highest, returned_best)
    returned = lax.all_to_all(
        highest.reshape(groups, capacity), "grp", split_axis=0, concat_axis=0, tiled=True
    )
    return returned.reshape(groups * capacity)[slot_index]


def unit(rows):
    floats = rows.astype(jnp.float32)
    square = jnp.mean(floats * floats, axis=1, keepdims=True)
    return (floats * lax.rsqrt(square + 1e-06) / math.sqrt(rows.shape[1])).astype(jnp.bfloat16)


def own_kernel(rows_hbm, names_hbm, own_ref, rows_ref, names_ref, arrived):
    size = rows_ref.shape[0]
    pieces = arrived.shape[0] - 1
    step = size // pieces
    copies = [
        pltpu.make_async_copy(
            rows_hbm.at[pl.ds(at * step, step)], rows_ref.at[pl.ds(at * step, step)], arrived.at[at]
        )
        for at in range(pieces)
    ]
    copies.append(pltpu.make_async_copy(names_hbm, names_ref, arrived.at[pieces]))
    for copy in copies:
        copy.start()
    for at in range(pieces):
        copies[at].wait()
        own_ref[at * step : (at + 1) * step] = unit(rows_ref[at * step : (at + 1) * step])
    copies[pieces].wait()
    names = names_ref[...].astype(jnp.float32).astype(jnp.bfloat16)
    names = jnp.concatenate(
        [names, jnp.zeros((1, own_ref.shape[1] - size), jnp.bfloat16)], axis=1
    )
    own_ref[size:] = jnp.broadcast_to(names, (own_ref.shape[0] - size, names.shape[1]))


def labels_in(ref, size):
    below = size if ref.shape[0] > size else size // 2
    return ref[below:][:1, :size].astype(jnp.float32)


def best_of(columns, row_labels, names, rows, skip_own=False):
    step = columns.shape[0]
    scores = lax.dot_general(
        columns, rows, (((1,), (1,)), ((), ())), preferred_element_type=jnp.float32
    )
    tall = jnp.broadcast_to(names, (128, step)).T
    tall = jnp.concatenate([tall] * (rows.shape[0] // 128), axis=1)
    allowed = tall == row_labels
    if skip_own:
        down = lax.broadcasted_iota(jnp.int32, scores.shape, 0)
        across = lax.broadcasted_iota(jnp.int32, scores.shape, 1)
        allowed = allowed & (down != across)
    return jnp.max(jnp.where(allowed, scores, -1.0), axis=0, keepdims=True)


def cut_kernel(parts, *refs):
    for whole_ref, half_ref, upper in zip(refs, refs[len(parts) :], parts):
        half = whole_ref.shape[0] // 2 // 16 * 16
        if upper:
            half_ref[:half] = whole_ref[:half]
            half_ref[half:] = whole_ref[2 * half :]
        else:
            half_ref[...] = whole_ref[half : 2 * half]


def columns_in(refs, size):
    refs, found = list(refs), []
    while refs:
        first = refs.pop(0)
        if first.shape[0] > size:
            found.append((first[:size], labels_in(first, size)))
        else:
            columns = jnp.concatenate([first[: size // 2], refs.pop(0)[...]], axis=0)
            found.append((columns, labels_in(first, size)))
    return found


def best_over(refs, rows, row_labels, size, best):
    for columns, names in columns_in(refs, size):
        best = jnp.maximum(best, best_of(columns, row_labels, names, rows))
    return best


def place_kernel(own_ref, core_ref, peer_ref, *refs):
    rows_ref, row_labels_ref, best_ref = refs[-3:]
    size = best_ref.shape[1] // 2
    own_labels = labels_in(own_ref, size)
    rows_ref[:size] = own_ref[:size]
    rows_ref[size:] = peer_ref[:size]
    row_labels_ref[:, :size] = own_labels
    row_labels_ref[:, size:] = labels_in(peer_ref, size)
    rows, row_labels = rows_ref[...], row_labels_ref[...]
    best = best_of(own_ref[:size], row_labels, own_labels, rows, True)
    best = jnp.maximum(best, -1.0)
    best_ref[...] = best_over((core_ref,) + refs[:-3], rows, row_labels, size, best)


def near_kernel(rows_ref, row_labels_ref, before_ref, *refs):
    size = row_labels_ref.shape[1] // 2
    refs[-1][...] = best_over(
        refs[:-1], rows_ref[...], row_labels_ref[...], size, before_ref[...]
    )


def far_kernel(far_ref, *refs):
    best_ref = refs[-1]
    size = best_ref.shape[1]
    best = jnp.full(best_ref.shape, -1.0, jnp.float32)
    best_ref[...] = best_over(refs[:-1], far_ref[:size], labels_in(far_ref, size), size, best)


def far_other_kernel(far_ref, before_ref, *refs):
    best_ref = refs[-1]
    size = best_ref.shape[1]
    best_ref[...] = best_over(
        refs[:-1], far_ref[:size], labels_in(far_ref, size), size, before_ref[...]
    )


def rows_kernel(rows_ref, row_labels_ref, before_ref, *refs):
    own_ref, peer_ref = refs[-2:]
    size = own_ref.shape[1]
    best = best_over(refs[:-2], rows_ref[...], row_labels_ref[...], size, before_ref[...])
    own_ref[...] = best[:, :size]
    peer_ref[...] = best[:, size:]


def larger_kernel(first_ref, second_ref, best_ref):
    best_ref[...] = jnp.maximum(first_ref[...], second_ref[...])


def call(kernel, outs, args, name, flops=1, **more):
    more.setdefault("in_specs", [VMEM] * len(args))
    return pl.pallas_call(
        kernel,
        out_shape=outs,
        out_specs=jax.tree.map(lambda _: VMEM, outs),
        compiler_params=pltpu.CompilerParams(vmem_limit_bytes=32 * 2**20),
        cost_estimate=flops and pl.CostEstimate(flops=flops, bytes_accessed=0, transcendentals=0),
        name=name,
        **more,
    )(*args)


def after(value, *others):
    return lax.optimization_barrier((value,) + others)[0]


def dense(embeddings, cluster_ids):
    rows_dev, features = embeddings.shape
    groups, subgroup = lax.axis_size("grp"), lax.axis_size("sub")
    half = rows_dev // 2
    bf16 = functools.partial(jax.ShapeDtypeStruct, dtype=jnp.bfloat16)
    f32 = functools.partial(jax.ShapeDtypeStruct, dtype=jnp.float32)
    inner = groups // 2

    def core(v):
        return lax.ppermute(v, "sub", [(s, s ^ 1) for s in range(subgroup)])

    def cross(v):
        return lax.ppermute(v, "sub", [(s, s ^ 2) for s in range(subgroup)])

    def beside(v):
        return lax.ppermute(v, "grp", [(g, g ^ 1) for g in range(groups)])

    def middle(v):
        pairs = []
        for g in range(groups):
            for s in range(subgroup):
                other = (groups - 1 - g, s) if g in (inner - 1, inner) else (g, s ^ 1)
                pairs.append((g * subgroup + s, other[0] * subgroup + other[1]))
        return lax.ppermute(v, ("grp", "sub"), pairs)

    def skip_one(v):
        return lax.ppermute(v, "grp", [(g, (g + inner) % groups) for g in range(groups)])

    extra = 8
    own = call(
        own_kernel,
        bf16((rows_dev + extra, features)),
        [
            pltpu.with_memory_space_constraint(v, pltpu.HBM)
            for v in (embeddings, cluster_ids[:, 0][None, :])
        ],
        "own_rows",
        in_specs=[pl.BlockSpec(memory_space=pltpu.HBM)] * 2,
        scratch_shapes=[
            pltpu.VMEM((rows_dev, features), embeddings.dtype),
            pltpu.VMEM((1, rows_dev), cluster_ids.dtype),
            pltpu.SemaphoreType.DMA((PIECES + 1,)),
        ],
    )
    near, peer, across = beside(own), middle(own), cross(own)
    pair = core(own)
    far = middle(near)
    upper_half, lower_half = bf16((half + extra, features)), bf16((half, features))
    near_upper, across_upper, across_lower = call(
        functools.partial(cut_kernel, (True, True, False)),
        (upper_half, upper_half, lower_half),
        (after(near, peer), across, across),
        "halves",
    )
    upper, lower = cross(near_upper), beside(across_lower)
    near_pair = [core(near)]
    across_pair = [core(v) for v in (across_upper, across_lower)]
    rows, row_labels, best = call(
        place_kernel,
        (bf16((2 * rows_dev, features)), f32((1, 2 * rows_dev)), f32((1, 2 * rows_dev))),
        [own, pair, peer, across] + across_pair,
        "own_place",
        1,
    )
    best = call(
        near_kernel,
        f32((1, 2 * rows_dev)),
        [rows, row_labels, best, near] + near_pair,
        "beside",
        1,
    )
    upper_pair = core(after(upper, best))
    lower_pair = core(after(lower, best))
    for_far = call(
        far_kernel,
        f32((1, rows_dev)),
        [far, own, pair, across] + across_pair + [near] + near_pair,
        "far_rows",
        5000000000,
    )
    for_far = call(
        far_other_kernel,
        f32((1, rows_dev)),
        [far, for_far, upper, lower, upper_pair, lower_pair],
        "far_rows_other",
    )
    from_far = skip_one(for_far)
    mine, for_peer = call(
        rows_kernel,
        (f32((1, rows_dev)),) * 2,
        (rows, row_labels, best, upper, lower, upper_pair, lower_pair),
        "beside_other",
    )
    from_peer = middle(for_peer)
    with_far = call(larger_kernel, f32((1, rows_dev)), (mine, from_far), "larger")
    place = lax.axis_index("grp")
    is_inner = (place == inner - 1) | (place == inner)
    return jnp.where(is_inner, jnp.maximum(mine, from_peer), with_far)[0]


def solution(mesh):
    fits = mesh.shape["grp"] == mesh.shape["sub"] == 2 * 2
    return jax.shard_map(
        dense if fits else clustered,
        mesh=mesh,
        in_specs=(P(("rep", "grp", "sub"), None), P(("rep", "grp", "sub"), None)),
        out_specs=P(("rep", "grp", "sub")),
        check_vma=False,
    )
```

```python
import functools
import math

import jax
import jax.numpy as jnp
from jax import lax
from jax.experimental import pallas as pl
from jax.experimental.pallas import tpu as pltpu
from jax.sharding import PartitionSpec as P

PIECES = 2
VMEM = pl.BlockSpec(memory_space=pltpu.VMEM)
SMEM = pl.BlockSpec(memory_space=pltpu.SMEM)


def from_behind(value, axis, by):
    peers = lax.axis_size(axis)
    return lax.ppermute(value, axis, [(i, (i + by) % peers) for i in range(peers)])


def masked_maxima(left_rows, right_rows, right_present, excluded):
    similar = jnp.dot(left_rows, right_rows.T, preferred_element_type=jnp.float32)
    allowed = (right_present[None, :] > 0) & jnp.logical_not(excluded)
    return jnp.where(allowed, similar, jnp.float32(-1.0))


def clustered(embeddings, cluster_ids):
    rows_dev, features = embeddings.shape
    groups = lax.axis_size("grp")
    subgroup = lax.axis_size("sub")
    capacity = 2 * rows_dev // groups
    unit_rows = unit(embeddings)
    labels = cluster_ids[:, 0]
    member_table = (labels[:, None] == jnp.arange(groups, dtype=jnp.int32)[None, :]).astype(
        jnp.int32
    )
    running = jnp.cumsum(member_table, axis=0)
    within = jnp.sum(jnp.where(member_table > 0, running - 1, 0), axis=1)
    slot_index = labels * capacity + within
    outgoing = jnp.zeros((groups * capacity, features), jnp.bfloat16).at[slot_index].set(unit_rows)
    occupied = jnp.zeros((groups * capacity,), jnp.int32).at[slot_index].set(1)
    arrived, arrived_present = (
        lax.all_to_all(
            outgoing.reshape(groups, capacity, features),
            "grp",
            split_axis=0,
            concat_axis=0,
            tiled=True,
        ),
        lax.all_to_all(
            occupied.reshape(groups, capacity), "grp", split_axis=0, concat_axis=0, tiled=True
        ),
    )
    owned_rows = arrived.reshape(groups * capacity, features)
    present = arrived_present.reshape(groups * capacity)
    held = owned_rows.shape[0]
    positions = jnp.arange(held, dtype=jnp.int32)
    excluded = positions[:, None] == positions[None, :]
    highest = jnp.max(masked_maxima(owned_rows, owned_rows, present, excluded), axis=1)
    no_exclusion = jnp.zeros((held, held), dtype=bool)
    for offset in range(1, subgroup // 2 + 1):
        peer_rows, peer_present = from_behind((owned_rows, present), "sub", offset)
        scores = masked_maxima(owned_rows, peer_rows, peer_present, no_exclusion)
        highest = jnp.maximum(highest, jnp.max(scores, axis=1))
        if 2 * offset != subgroup:
            column_best = jnp.max(
                jnp.where(present[:, None] > 0, scores, jnp.float32(-1.0)), axis=0
            )
            returned_best = from_behind(column_best, "sub", -offset)
            highest = jnp.maximum(highest, returned_best)
    returned = lax.all_to_all(
        highest.reshape(groups, capacity), "grp", split_axis=0, concat_axis=0, tiled=True
    )
    return returned.reshape(groups * capacity)[slot_index]


def unit(rows):
    floats = rows.astype(jnp.float32)
    square = jnp.mean(floats * floats, axis=1, keepdims=True)
    return (floats * lax.rsqrt(square + 1e-06) / math.sqrt(rows.shape[1])).astype(jnp.bfloat16)


def own_kernel(rows_hbm, names_hbm, own_ref, rows_ref, names_ref, arrived):
    size = rows_ref.shape[0]
    pieces = arrived.shape[0] - 1
    step = size // pieces
    copies = [
        pltpu.make_async_copy(
            rows_hbm.at[pl.ds(at * step, step)], rows_ref.at[pl.ds(at * step, step)], arrived.at[at]
        )
        for at in range(pieces)
    ]
    copies.append(pltpu.make_async_copy(names_hbm, names_ref, arrived.at[pieces]))
    for copy in copies:
        copy.start()
    for at in range(pieces):
        copies[at].wait()
        own_ref[at * step : (at + 1) * step] = unit(rows_ref[at * step : (at + 1) * step])
    copies[pieces].wait()
    names = names_ref[...].astype(jnp.float32).astype(jnp.bfloat16)
    names = jnp.concatenate(
        [names, jnp.zeros((1, own_ref.shape[1] - size), jnp.bfloat16)], axis=1
    )
    own_ref[size:] = jnp.broadcast_to(names, (own_ref.shape[0] - size, names.shape[1]))


def labels_in(ref, size):
    return ref[ref.shape[0] // 16 * 16 :][:1, :size].astype(jnp.float32)


def best_of(columns, row_labels, names, rows, skip_own=False):
    step = columns.shape[0]
    scores = lax.dot_general(
        columns, rows, (((1,), (1,)), ((), ())), preferred_element_type=jnp.float32
    )
    tall = jnp.broadcast_to(names, (128, step)).T
    tall = jnp.concatenate([tall] * (rows.shape[0] // 128), axis=1)
    allowed = tall == row_labels
    if skip_own:
        down = lax.broadcasted_iota(jnp.int32, scores.shape, 0)
        across = lax.broadcasted_iota(jnp.int32, scores.shape, 1)
        allowed = allowed & (down != across)
    return jnp.max(jnp.where(allowed, scores, -1.0), axis=0, keepdims=True)


def cut_kernel(parts, *refs):
    for whole_ref, part_ref, (at, count) in zip(refs, refs[len(parts) :], parts):
        size = whole_ref.shape[0] // 16 * 16
        rows = size // count
        part_ref[:rows] = whole_ref[at * rows : (at + 1) * rows]
        if at == 0:
            part_ref[rows:] = whole_ref[size:]


def join_kernel(upper_ref, lower_ref, whole_ref):
    half = lower_ref.shape[0]
    whole_ref[:half] = upper_ref[:half]
    whole_ref[half : 2 * half] = lower_ref[...]
    whole_ref[2 * half :] = upper_ref[half:]


def columns_in(refs, size):
    refs, found = list(refs), []
    while refs:
        parts = [refs.pop(0)]
        rows = parts[0].shape[0] // 16 * 16
        names = labels_in(parts[0], size)
        while len(parts) * rows < size:
            parts.append(refs.pop(0))
        columns = [part[:rows] for part in parts]
        found.append((columns[0] if rows == size else jnp.concatenate(columns, axis=0), names))
    return found


def best_over(refs, rows, row_labels, size, best):
    for columns, names in columns_in(refs, size):
        best = jnp.maximum(best, best_of(columns, row_labels, names, rows))
    return best


def place_kernel(own_ref, core_ref, peer_ref, *refs):
    rows_ref, row_labels_ref, best_ref = refs[-3:]
    size = best_ref.shape[1] // 2
    own_labels = labels_in(own_ref, size)
    rows_ref[:size] = own_ref[:size]
    rows_ref[size:] = peer_ref[:size]
    row_labels_ref[:, :size] = own_labels
    row_labels_ref[:, size:] = labels_in(peer_ref, size)
    rows, row_labels = rows_ref[...], row_labels_ref[...]
    best = best_of(own_ref[:size], row_labels, own_labels, rows, True)
    best = jnp.maximum(best, -1.0)
    best_ref[...] = best_over((core_ref,) + refs[:-3], rows, row_labels, size, best)


def near_kernel(rows_ref, row_labels_ref, before_ref, *refs):
    size = row_labels_ref.shape[1] // 2
    refs[-1][...] = best_over(
        refs[:-1], rows_ref[...], row_labels_ref[...], size, before_ref[...]
    )


def far_kernel(far_ref, rows_ref, row_labels_ref, before_ref, *refs):
    far_best_ref, best_ref = refs[-2:]
    size = far_best_ref.shape[1]
    far_best = jnp.full(far_best_ref.shape, -1.0, jnp.float32)
    far_best_ref[...] = best_over(
        refs[:-2], far_ref[:size], labels_in(far_ref, size), size, far_best
    )
    best_ref[...] = best_over(
        refs[-3:-2], rows_ref[...], row_labels_ref[...], size, before_ref[...]
    )


def far_other_kernel(far_ref, before_ref, *refs):
    best_ref = refs[-1]
    size = best_ref.shape[1]
    best_ref[...] = best_over(
        refs[:-1], far_ref[:size], labels_in(far_ref, size), size, before_ref[...]
    )


def rows_kernel(rows_ref, row_labels_ref, before_ref, *refs):
    own_ref, peer_ref = refs[-2:]
    size = own_ref.shape[1]
    best = best_over(refs[:-2], rows_ref[...], row_labels_ref[...], size, before_ref[...])
    own_ref[...] = best[:, :size]
    peer_ref[...] = best[:, size:]


def larger_kernel(first_ref, second_ref, best_ref):
    best_ref[...] = jnp.maximum(first_ref[...], second_ref[...])


def call(kernel, outs, args, name, flops=1, **more):
    more.setdefault("in_specs", [VMEM] * len(args))
    return pl.pallas_call(
        kernel,
        out_shape=outs,
        out_specs=jax.tree.map(lambda _: VMEM, outs),
        compiler_params=pltpu.CompilerParams(vmem_limit_bytes=32 * 2**20),
        cost_estimate=flops and pl.CostEstimate(flops=flops, bytes_accessed=0, transcendentals=0),
        name=name,
        **more,
    )(*args)


def after(value, *others):
    return lax.optimization_barrier((value,) + others)[0]


def dense(embeddings, cluster_ids):
    rows_dev, features = embeddings.shape
    groups, subgroup = lax.axis_size("grp"), lax.axis_size("sub")
    half = rows_dev // 2
    bf16 = functools.partial(jax.ShapeDtypeStruct, dtype=jnp.bfloat16)
    f32 = functools.partial(jax.ShapeDtypeStruct, dtype=jnp.float32)
    inner = groups // 2

    def core(v):
        return lax.ppermute(v, "sub", [(s, s ^ 1) for s in range(subgroup)])

    def cross(v):
        return lax.ppermute(v, "sub", [(s, s ^ 2) for s in range(subgroup)])

    def beside(v):
        return lax.ppermute(v, "grp", [(g, g ^ 1) for g in range(groups)])

    def middle(v):
        pairs = []
        for g in range(groups):
            for s in range(subgroup):
                other = (groups - 1 - g, s) if g in (inner - 1, inner) else (g, s ^ 1)
                pairs.append((g * subgroup + s, other[0] * subgroup + other[1]))
        return lax.ppermute(v, ("grp", "sub"), pairs)

    def skip_one(v):
        return lax.ppermute(v, "grp", [(g, (g + inner) % groups) for g in range(groups)])

    extra = 8
    own = call(
        own_kernel,
        bf16((rows_dev + extra, features)),
        [
            pltpu.with_memory_space_constraint(v, pltpu.HBM)
            for v in (embeddings, cluster_ids[:, 0][None, :])
        ],
        "own_rows",
        in_specs=[pl.BlockSpec(memory_space=pltpu.HBM)] * 2,
        scratch_shapes=[
            pltpu.VMEM((rows_dev, features), embeddings.dtype),
            pltpu.VMEM((1, rows_dev), cluster_ids.dtype),
            pltpu.SemaphoreType.DMA((PIECES + 1,)),
        ],
    )
    near, peer, across = beside(own), middle(own), cross(own)
    pair = core(own)
    far = middle(near)
    upper_half, lower_half = bf16((half + extra, features)), bf16((half, features))
    near_upper, near_lower, across_lower = call(
        functools.partial(cut_kernel, ((0, 2), (1, 2), (1, 2))),
        (upper_half, lower_half, lower_half),
        (after(near, peer), after(near, peer), after(across, peer)),
        "halves",
    )
    upper, lower = cross(near_upper), beside(across_lower)
    near_pair = [core(v) for v in (near_upper, near_lower)]
    across_pair = [core(across)]
    rows, row_labels, best0 = call(
        place_kernel,
        (bf16((2 * rows_dev, features)), f32((1, 2 * rows_dev)), f32((1, 2 * rows_dev))),
        [own, pair, peer, across, near],
        "own_place",
        1,
    )
    other = call(join_kernel, bf16((rows_dev + extra, features)), (upper, lower), "other", 1)
    best1 = call(
        near_kernel,
        f32((1, 2 * rows_dev)),
        [after(rows, other), row_labels, best0] + near_pair,
        "beside",
        1,
    )
    other_pair = core(after(other, best1))
    for_far, best2 = call(
        far_kernel,
        (f32((1, rows_dev)), f32((1, 2 * rows_dev))),
        [far, rows, row_labels, best1, own, pair, across, near] + near_pair + across_pair,
        "far_rows",
        8000000000,
    )
    for_far = call(
        far_other_kernel,
        f32((1, rows_dev)),
        [far, for_far, other, other_pair],
        "far_rows_other",
    )
    from_far = skip_one(for_far)
    mine, for_peer = call(
        rows_kernel,
        (f32((1, rows_dev)),) * 2,
        (rows, row_labels, best2, other, other_pair),
        "beside_other",
    )
    from_peer = middle(for_peer)
    with_far = call(larger_kernel, f32((1, rows_dev)), (mine, from_far), "larger")
    place = lax.axis_index("grp")
    is_inner = (place == inner - 1) | (place == inner)
    return jnp.where(is_inner, jnp.maximum(mine, from_peer), with_far)[0]


def solution(mesh):
    fits = mesh.shape["grp"] == mesh.shape["sub"] == 2 * 2
    return jax.shard_map(
        dense if fits else clustered,
        mesh=mesh,
        in_specs=(P(("rep", "grp", "sub"), None), P(("rep", "grp", "sub"), None)),
        out_specs=P(("rep", "grp", "sub")),
        check_vma=False,
    )
```

```python
import functools
import math

import jax
import jax.numpy as jnp
from jax import lax
from jax.experimental import pallas as pl
from jax.experimental.pallas import tpu as pltpu
from jax.sharding import PartitionSpec as P

PIECES = 1
VMEM = pl.BlockSpec(memory_space=pltpu.VMEM)
SMEM = pl.BlockSpec(memory_space=pltpu.SMEM)


def from_behind(value, axis, by):
    peers = lax.axis_size(axis)
    return lax.ppermute(value, axis, [(i, (i + by) % peers) for i in range(peers)])


def masked_maxima(left_rows, right_rows, right_present, excluded):
    similar = jnp.dot(left_rows, right_rows.T, preferred_element_type=jnp.float32)
    allowed = (right_present[None, :] > 0) & jnp.logical_not(excluded)
    return jnp.where(allowed, similar, jnp.float32(-1.0))


def clustered(embeddings, cluster_ids):
    rows_dev, features = embeddings.shape
    groups = lax.axis_size("grp")
    subgroup = lax.axis_size("sub")
    capacity = 2 * rows_dev // groups
    unit_rows = unit(embeddings)
    labels = cluster_ids[:, 0]
    member_table = (labels[:, None] == jnp.arange(groups, dtype=jnp.int32)[None, :]).astype(
        jnp.int32
    )
    running = jnp.cumsum(member_table, axis=0)
    within = jnp.sum(jnp.where(member_table > 0, running - 1, 0), axis=1)
    slot_index = labels * capacity + within
    outgoing = jnp.zeros((groups * capacity, features), jnp.bfloat16).at[slot_index].set(unit_rows)
    occupied = jnp.zeros((groups * capacity,), jnp.int32).at[slot_index].set(1)
    arrived, arrived_present = (
        lax.all_to_all(
            outgoing.reshape(groups, capacity, features),
            "grp",
            split_axis=0,
            concat_axis=0,
            tiled=True,
        ),
        lax.all_to_all(
            occupied.reshape(groups, capacity), "grp", split_axis=0, concat_axis=0, tiled=True
        ),
    )
    owned_rows = arrived.reshape(groups * capacity, features)
    present = arrived_present.reshape(groups * capacity)
    held = owned_rows.shape[0]
    positions = jnp.arange(held, dtype=jnp.int32)
    excluded = positions[:, None] == positions[None, :]
    highest = jnp.max(masked_maxima(owned_rows, owned_rows, present, excluded), axis=1)
    no_exclusion = jnp.zeros((held, held), dtype=bool)
    for offset in range(1, subgroup // 2 + 1):
        peer_rows, peer_present = from_behind((owned_rows, present), "sub", offset)
        scores = masked_maxima(owned_rows, peer_rows, peer_present, no_exclusion)
        highest = jnp.maximum(highest, jnp.max(scores, axis=1))
        if 2 * offset != subgroup:
            column_best = jnp.max(
                jnp.where(present[:, None] > 0, scores, jnp.float32(-1.0)), axis=0
            )
            returned_best = from_behind(column_best, "sub", -offset)
            highest = jnp.maximum(highest, returned_best)
    returned = lax.all_to_all(
        highest.reshape(groups, capacity), "grp", split_axis=0, concat_axis=0, tiled=True
    )
    return returned.reshape(groups * capacity)[slot_index]


def unit(rows):
    floats = rows.astype(jnp.float32)
    square = jnp.mean(floats * floats, axis=1, keepdims=True)
    return (floats * lax.rsqrt(square + 1e-06) / math.sqrt(rows.shape[1])).astype(jnp.bfloat16)


def own_kernel(rows_hbm, names_hbm, own_ref, rows_ref, names_ref, arrived):
    size = rows_ref.shape[0]
    pieces = arrived.shape[0] - 1
    step = size // pieces
    copies = [
        pltpu.make_async_copy(
            rows_hbm.at[pl.ds(at * step, step)], rows_ref.at[pl.ds(at * step, step)], arrived.at[at]
        )
        for at in range(pieces)
    ]
    copies.append(pltpu.make_async_copy(names_hbm, names_ref, arrived.at[pieces]))
    for copy in copies:
        copy.start()
    for at in range(pieces):
        copies[at].wait()
        own_ref[at * step : (at + 1) * step] = unit(rows_ref[at * step : (at + 1) * step])
    copies[pieces].wait()
    names = names_ref[...].astype(jnp.float32).astype(jnp.bfloat16)
    names = jnp.concatenate(
        [names, jnp.zeros((1, own_ref.shape[1] - size), jnp.bfloat16)], axis=1
    )
    own_ref[size:] = jnp.broadcast_to(names, (own_ref.shape[0] - size, names.shape[1]))


def labels_in(ref, size):
    return ref[ref.shape[0] // 16 * 16 :][:1, :size].astype(jnp.float32)


def best_of(columns, row_labels, names, rows, skip_own=False):
    step = columns.shape[0]
    scores = lax.dot_general(
        columns, rows, (((1,), (1,)), ((), ())), preferred_element_type=jnp.float32
    )
    tall = jnp.broadcast_to(names, (128, step)).T
    tall = jnp.concatenate([tall] * (rows.shape[0] // 128), axis=1)
    allowed = tall == row_labels
    if skip_own:
        down = lax.broadcasted_iota(jnp.int32, scores.shape, 0)
        across = lax.broadcasted_iota(jnp.int32, scores.shape, 1)
        allowed = allowed & (down != across)
    return jnp.max(jnp.where(allowed, scores, -1.0), axis=0, keepdims=True)


def cut_kernel(parts, *refs):
    for whole_ref, part_ref, (at, count) in zip(refs, refs[len(parts) :], parts):
        size = whole_ref.shape[0] // 16 * 16
        rows = size // count
        part_ref[:rows] = whole_ref[at * rows : (at + 1) * rows]
        if at == 0:
            part_ref[rows:] = whole_ref[size:]


def join_kernel(upper_ref, lower_ref, whole_ref):
    half = lower_ref.shape[0]
    whole_ref[:half] = upper_ref[:half]
    whole_ref[half : 2 * half] = lower_ref[...]
    whole_ref[2 * half :] = upper_ref[half:]


def columns_in(refs, size):
    refs, found = list(refs), []
    while refs:
        parts = [refs.pop(0)]
        rows = parts[0].shape[0] // 16 * 16
        names = labels_in(parts[0], size)
        while len(parts) * rows < size:
            parts.append(refs.pop(0))
        columns = [part[:rows] for part in parts]
        found.append((columns[0] if rows == size else jnp.concatenate(columns, axis=0), names))
    return found


def best_over(refs, rows, row_labels, size, best):
    for columns, names in columns_in(refs, size):
        best = jnp.maximum(best, best_of(columns, row_labels, names, rows))
    return best


def place_kernel(own_ref, core_ref, peer_ref, *refs):
    rows_ref, row_labels_ref, best_ref = refs[-3:]
    size = best_ref.shape[1] // 2
    own_labels = labels_in(own_ref, size)
    rows_ref[:size] = own_ref[:size]
    rows_ref[size:] = peer_ref[:size]
    row_labels_ref[:, :size] = own_labels
    row_labels_ref[:, size:] = labels_in(peer_ref, size)
    rows, row_labels = rows_ref[...], row_labels_ref[...]
    best = best_of(own_ref[:size], row_labels, own_labels, rows, True)
    best = jnp.maximum(best, -1.0)
    best_ref[...] = best_over((core_ref,) + refs[:-3], rows, row_labels, size, best)


def near_kernel(rows_ref, row_labels_ref, before_ref, *refs):
    size = row_labels_ref.shape[1] // 2
    refs[-1][...] = best_over(
        refs[:-1], rows_ref[...], row_labels_ref[...], size, before_ref[...]
    )


def far_kernel(far_ref, rows_ref, row_labels_ref, before_ref, *refs):
    far_best_ref, best_ref = refs[-2:]
    size = far_best_ref.shape[1]
    far_best = jnp.full(far_best_ref.shape, -1.0, jnp.float32)
    far_best_ref[...] = best_over(
        refs[:-2], far_ref[:size], labels_in(far_ref, size), size, far_best
    )
    best_ref[...] = best_over(
        refs[-3:-2], rows_ref[...], row_labels_ref[...], size, before_ref[...]
    )


def far_other_kernel(far_ref, before_ref, *refs):
    best_ref = refs[-1]
    size = best_ref.shape[1]
    best_ref[...] = best_over(
        refs[:-1], far_ref[:size], labels_in(far_ref, size), size, before_ref[...]
    )


def rows_kernel(which, rows_ref, row_labels_ref, before_ref, *refs):
    best_ref = refs[-1]
    size = best_ref.shape[1]
    mine = slice(which * size, (which + 1) * size)
    best_ref[...] = best_over(
        refs[:-1], rows_ref[mine], row_labels_ref[:, mine], size, before_ref[:, mine]
    )


def larger_kernel(first_ref, second_ref, best_ref):
    best_ref[...] = jnp.maximum(first_ref[...], second_ref[...])


def call(kernel, outs, args, name, flops=1, **more):
    more.setdefault("in_specs", [VMEM] * len(args))
    return pl.pallas_call(
        kernel,
        out_shape=outs,
        out_specs=jax.tree.map(lambda _: VMEM, outs),
        compiler_params=pltpu.CompilerParams(vmem_limit_bytes=32 * 2**20),
        cost_estimate=flops and pl.CostEstimate(flops=flops, bytes_accessed=0, transcendentals=0),
        name=name,
        **more,
    )(*args)


def after(value, *others):
    return lax.optimization_barrier((value,) + others)[0]


def dense(embeddings, cluster_ids):
    rows_dev, features = embeddings.shape
    groups, subgroup = lax.axis_size("grp"), lax.axis_size("sub")
    half = rows_dev // 2
    bf16 = functools.partial(jax.ShapeDtypeStruct, dtype=jnp.bfloat16)
    f32 = functools.partial(jax.ShapeDtypeStruct, dtype=jnp.float32)
    inner = groups // 2

    def core(v):
        return lax.ppermute(v, "sub", [(s, s ^ 1) for s in range(subgroup)])

    def cross(v):
        return lax.ppermute(v, "sub", [(s, s ^ 2) for s in range(subgroup)])

    def beside(v):
        return lax.ppermute(v, "grp", [(g, g ^ 1) for g in range(groups)])

    def middle(v):
        pairs = []
        for g in range(groups):
            for s in range(subgroup):
                other = (groups - 1 - g, s) if g in (inner - 1, inner) else (g, s ^ 1)
                pairs.append((g * subgroup + s, other[0] * subgroup + other[1]))
        return lax.ppermute(v, ("grp", "sub"), pairs)

    def skip_one(v):
        return lax.ppermute(v, "grp", [(g, (g + inner) % groups) for g in range(groups)])

    extra = 8
    own = call(
        own_kernel,
        bf16((rows_dev + extra, features)),
        [
            pltpu.with_memory_space_constraint(v, pltpu.HBM)
            for v in (embeddings, cluster_ids[:, 0][None, :])
        ],
        "own_rows",
        in_specs=[pl.BlockSpec(memory_space=pltpu.HBM)] * 2,
        scratch_shapes=[
            pltpu.VMEM((rows_dev, features), embeddings.dtype),
            pltpu.VMEM((1, rows_dev), cluster_ids.dtype),
            pltpu.SemaphoreType.DMA((PIECES + 1,)),
        ],
    )
    near, peer, across = beside(own), middle(own), cross(own)
    pair = core(own)
    far = middle(near)
    upper_half, lower_half = bf16((half + extra, features)), bf16((half, features))
    near_upper, near_lower, across_lower = call(
        functools.partial(cut_kernel, ((0, 2), (1, 2), (1, 2))),
        (upper_half, lower_half, lower_half),
        (after(near, peer), after(near, peer), after(across, peer)),
        "halves",
    )
    upper, lower = cross(near_upper), beside(across_lower)
    near_pair = [core(v) for v in (near_upper, near_lower)]
    across_pair = [core(across)]
    rows, row_labels, best0 = call(
        place_kernel,
        (bf16((2 * rows_dev, features)), f32((1, 2 * rows_dev)), f32((1, 2 * rows_dev))),
        [own, pair, peer, across, near],
        "own_place",
        1,
    )
    other = call(join_kernel, bf16((rows_dev + extra, features)), (upper, lower), "other", 1)
    best1 = call(
        near_kernel,
        f32((1, 2 * rows_dev)),
        [after(rows, other), row_labels, best0] + near_pair,
        "beside",
        1,
    )
    other_pair = core(after(other, best1))
    for_far, best2 = call(
        far_kernel,
        (f32((1, rows_dev)), f32((1, 2 * rows_dev))),
        [far, rows, row_labels, best1, own, pair, across, near] + near_pair + across_pair,
        "far_rows",
        8000000000,
    )
    for_far = call(
        far_other_kernel,
        f32((1, rows_dev)),
        [far, for_far, other, other_pair],
        "far_rows_other",
    )
    from_far = skip_one(for_far)
    mine, for_peer = [
        call(
            functools.partial(rows_kernel, which),
            f32((1, rows_dev)),
            (rows, row_labels, best2, other, other_pair),
            name,
        )
        for which, name in enumerate(("own_other", "peer_other"))
    ]
    from_peer = middle(for_peer)
    with_far = call(larger_kernel, f32((1, rows_dev)), (mine, from_far), "larger")
    place = lax.axis_index("grp")
    is_inner = (place == inner - 1) | (place == inner)
    return jnp.where(is_inner, jnp.maximum(mine, from_peer), with_far)[0]


def solution(mesh):
    fits = mesh.shape["grp"] == mesh.shape["sub"] == 2 * 2
    return jax.shard_map(
        dense if fits else clustered,
        mesh=mesh,
        in_specs=(P(("rep", "grp", "sub"), None), P(("rep", "grp", "sub"), None)),
        out_specs=P(("rep", "grp", "sub")),
        check_vma=False,
    )
```

```python
import functools
import math

import jax
import jax.numpy as jnp
from jax import lax
from jax.experimental import pallas as pl
from jax.experimental.pallas import tpu as pltpu
from jax.sharding import PartitionSpec as P

PIECES = 1
VMEM = pl.BlockSpec(memory_space=pltpu.VMEM)
SMEM = pl.BlockSpec(memory_space=pltpu.SMEM)


def from_behind(value, axis, by):
    peers = lax.axis_size(axis)
    return lax.ppermute(value, axis, [(i, (i + by) % peers) for i in range(peers)])


def masked_maxima(left_rows, right_rows, right_present, excluded):
    similar = jnp.dot(left_rows, right_rows.T, preferred_element_type=jnp.float32)
    allowed = (right_present[None, :] > 0) & jnp.logical_not(excluded)
    return jnp.where(allowed, similar, jnp.float32(-1.0))


def clustered(embeddings, cluster_ids):
    rows_dev, features = embeddings.shape
    groups = lax.axis_size("grp")
    subgroup = lax.axis_size("sub")
    capacity = 2 * rows_dev // groups
    unit_rows = unit(embeddings)
    labels = cluster_ids[:, 0]
    member_table = (labels[:, None] == jnp.arange(groups, dtype=jnp.int32)[None, :]).astype(
        jnp.int32
    )
    running = jnp.cumsum(member_table, axis=0)
    within = jnp.sum(jnp.where(member_table > 0, running - 1, 0), axis=1)
    slot_index = labels * capacity + within
    outgoing = jnp.zeros((groups * capacity, features), jnp.bfloat16).at[slot_index].set(unit_rows)
    occupied = jnp.zeros((groups * capacity,), jnp.int32).at[slot_index].set(1)
    arrived, arrived_present = (
        lax.all_to_all(
            outgoing.reshape(groups, capacity, features),
            "grp",
            split_axis=0,
            concat_axis=0,
            tiled=True,
        ),
        lax.all_to_all(
            occupied.reshape(groups, capacity), "grp", split_axis=0, concat_axis=0, tiled=True
        ),
    )
    owned_rows = arrived.reshape(groups * capacity, features)
    present = arrived_present.reshape(groups * capacity)
    held = owned_rows.shape[0]
    positions = jnp.arange(held, dtype=jnp.int32)
    excluded = positions[:, None] == positions[None, :]
    highest = jnp.max(masked_maxima(owned_rows, owned_rows, present, excluded), axis=1)
    no_exclusion = jnp.zeros((held, held), dtype=bool)
    for offset in range(1, subgroup // 2 + 1):
        peer_rows, peer_present = from_behind((owned_rows, present), "sub", offset)
        scores = masked_maxima(owned_rows, peer_rows, peer_present, no_exclusion)
        highest = jnp.maximum(highest, jnp.max(scores, axis=1))
        if 2 * offset != subgroup:
            column_best = jnp.max(
                jnp.where(present[:, None] > 0, scores, jnp.float32(-1.0)), axis=0
            )
            returned_best = from_behind(column_best, "sub", -offset)
            highest = jnp.maximum(highest, returned_best)
    returned = lax.all_to_all(
        highest.reshape(groups, capacity), "grp", split_axis=0, concat_axis=0, tiled=True
    )
    return returned.reshape(groups * capacity)[slot_index]


def unit(rows):
    floats = rows.astype(jnp.float32)
    square = jnp.mean(floats * floats, axis=1, keepdims=True)
    return (floats * lax.rsqrt(square + 1e-06) / math.sqrt(rows.shape[1])).astype(jnp.bfloat16)


def own_kernel(rows_hbm, names_hbm, own_ref, rows_ref, names_ref, arrived):
    size = rows_ref.shape[0]
    pieces = arrived.shape[0] - 1
    step = size // pieces
    copies = [
        pltpu.make_async_copy(
            rows_hbm.at[pl.ds(at * step, step)], rows_ref.at[pl.ds(at * step, step)], arrived.at[at]
        )
        for at in range(pieces)
    ]
    copies.append(pltpu.make_async_copy(names_hbm, names_ref, arrived.at[pieces]))
    for copy in copies:
        copy.start()
    for at in range(pieces):
        copies[at].wait()
        own_ref[at * step : (at + 1) * step] = unit(rows_ref[at * step : (at + 1) * step])
    copies[pieces].wait()
    names = names_ref[...].astype(jnp.float32).astype(jnp.bfloat16)
    names = jnp.concatenate(
        [names, jnp.zeros((1, own_ref.shape[1] - size), jnp.bfloat16)], axis=1
    )
    own_ref[size:] = jnp.broadcast_to(names, (own_ref.shape[0] - size, names.shape[1]))


def labels_in(ref, size):
    return ref[ref.shape[0] // 16 * 16 :][:1, :size].astype(jnp.float32)


def best_of(columns, row_labels, names, rows, skip_own=False):
    step = columns.shape[0]
    scores = lax.dot_general(
        columns, rows, (((1,), (1,)), ((), ())), preferred_element_type=jnp.float32
    )
    tall = jnp.broadcast_to(names, (128, step)).T
    tall = jnp.concatenate([tall] * (rows.shape[0] // 128), axis=1)
    allowed = tall == row_labels
    if skip_own:
        down = lax.broadcasted_iota(jnp.int32, scores.shape, 0)
        across = lax.broadcasted_iota(jnp.int32, scores.shape, 1)
        allowed = allowed & (down != across)
    return jnp.max(jnp.where(allowed, scores, -1.0), axis=0, keepdims=True)


def cut_kernel(parts, *refs):
    for whole_ref, part_ref, (at, count) in zip(refs, refs[len(parts) :], parts):
        size = whole_ref.shape[0] // 16 * 16
        rows = size // count
        part_ref[:rows] = whole_ref[at * rows : (at + 1) * rows]
        if at == 0:
            part_ref[rows:] = whole_ref[size:]


def join_kernel(upper_ref, lower_ref, whole_ref):
    half = lower_ref.shape[0]
    whole_ref[:half] = upper_ref[:half]
    whole_ref[half : 2 * half] = lower_ref[...]
    whole_ref[2 * half :] = upper_ref[half:]


def columns_in(refs, size):
    refs, found = list(refs), []
    while refs:
        parts = [refs.pop(0)]
        rows = parts[0].shape[0] // 16 * 16
        names = labels_in(parts[0], size)
        while len(parts) * rows < size:
            parts.append(refs.pop(0))
        columns = [part[:rows] for part in parts]
        found.append((columns[0] if rows == size else jnp.concatenate(columns, axis=0), names))
    return found


def best_over(refs, rows, row_labels, size, best):
    for columns, names in columns_in(refs, size):
        best = jnp.maximum(best, best_of(columns, row_labels, names, rows))
    return best


def place_kernel(own_ref, core_ref, peer_ref, *refs):
    rows_ref, row_labels_ref, best_ref = refs[-3:]
    size = best_ref.shape[1] // 2
    own_labels = labels_in(own_ref, size)
    rows_ref[:size] = own_ref[:size]
    rows_ref[size:] = peer_ref[:size]
    row_labels_ref[:, :size] = own_labels
    row_labels_ref[:, size:] = labels_in(peer_ref, size)
    rows, row_labels = rows_ref[...], row_labels_ref[...]
    best = best_of(own_ref[:size], row_labels, own_labels, rows, True)
    best = jnp.maximum(best, -1.0)
    best_ref[...] = best_over((core_ref,) + refs[:-3], rows, row_labels, size, best)


def near_kernel(rows_ref, row_labels_ref, before_ref, *refs):
    size = row_labels_ref.shape[1] // 2
    refs[-1][...] = best_over(
        refs[:-1], rows_ref[...], row_labels_ref[...], size, before_ref[...]
    )


def far_kernel(far_ref, *refs):
    best_ref, last_ref = refs[-2:]
    size = best_ref.shape[1]
    last_ref[...] = refs[-3][...]
    best = jnp.full(best_ref.shape, -1.0, jnp.float32)
    best_ref[...] = best_over(refs[:-2], far_ref[:size], labels_in(far_ref, size), size, best)


def far_other_kernel(far_ref, before_ref, *refs):
    best_ref = refs[-1]
    size = best_ref.shape[1]
    best_ref[...] = best_over(
        refs[:-1], far_ref[:size], labels_in(far_ref, size), size, before_ref[...]
    )


def rows_kernel(which, rows_ref, row_labels_ref, before_ref, *refs):
    best_ref = refs[-1]
    size = best_ref.shape[1]
    mine = slice(which * size, (which + 1) * size)
    best_ref[...] = best_over(
        refs[:-1], rows_ref[mine], row_labels_ref[:, mine], size, before_ref[:, mine]
    )


def larger_kernel(first_ref, second_ref, best_ref):
    best_ref[...] = jnp.maximum(first_ref[...], second_ref[...])


def call(kernel, outs, args, name, flops=1, **more):
    more.setdefault("in_specs", [VMEM] * len(args))
    return pl.pallas_call(
        kernel,
        out_shape=outs,
        out_specs=jax.tree.map(lambda _: VMEM, outs),
        compiler_params=pltpu.CompilerParams(vmem_limit_bytes=32 * 2**20),
        cost_estimate=flops and pl.CostEstimate(flops=flops, bytes_accessed=0, transcendentals=0),
        name=name,
        **more,
    )(*args)


def after(value, *others):
    return lax.optimization_barrier((value,) + others)[0]


def dense(embeddings, cluster_ids):
    rows_dev, features = embeddings.shape
    groups, subgroup = lax.axis_size("grp"), lax.axis_size("sub")
    half = rows_dev // 2
    bf16 = functools.partial(jax.ShapeDtypeStruct, dtype=jnp.bfloat16)
    f32 = functools.partial(jax.ShapeDtypeStruct, dtype=jnp.float32)
    inner = groups // 2

    def core(v):
        return lax.ppermute(v, "sub", [(s, s ^ 1) for s in range(subgroup)])

    def cross(v):
        return lax.ppermute(v, "sub", [(s, s ^ 2) for s in range(subgroup)])

    def beside(v):
        return lax.ppermute(v, "grp", [(g, g ^ 1) for g in range(groups)])

    def middle(v):
        pairs = []
        for g in range(groups):
            for s in range(subgroup):
                other = (groups - 1 - g, s) if g in (inner - 1, inner) else (g, s ^ 1)
                pairs.append((g * subgroup + s, other[0] * subgroup + other[1]))
        return lax.ppermute(v, ("grp", "sub"), pairs)

    def skip_one(v):
        return lax.ppermute(v, "grp", [(g, (g + inner) % groups) for g in range(groups)])

    extra = 8
    own = call(
        own_kernel,
        bf16((rows_dev + extra, features)),
        [
            pltpu.with_memory_space_constraint(v, pltpu.HBM)
            for v in (embeddings, cluster_ids[:, 0][None, :])
        ],
        "own_rows",
        in_specs=[pl.BlockSpec(memory_space=pltpu.HBM)] * 2,
        scratch_shapes=[
            pltpu.VMEM((rows_dev, features), embeddings.dtype),
            pltpu.VMEM((1, rows_dev), cluster_ids.dtype),
            pltpu.SemaphoreType.DMA((PIECES + 1,)),
        ],
    )
    near, peer, across = beside(own), middle(own), cross(own)
    pair = core(own)
    far = middle(near)
    upper_half, lower_half = bf16((half + extra, features)), bf16((half, features))
    near_upper, near_lower, across_lower = call(
        functools.partial(cut_kernel, ((0, 2), (1, 2), (1, 2))),
        (upper_half, lower_half, lower_half),
        (after(near, peer), after(near, peer), after(across, peer)),
        "halves",
    )
    upper, lower = cross(near_upper), beside(across_lower)
    near_pair = [core(v) for v in (near_upper, near_lower)]
    across_pair = [core(across)]
    rows, row_labels, best0 = call(
        place_kernel,
        (bf16((2 * rows_dev, features)), f32((1, 2 * rows_dev)), f32((1, 2 * rows_dev))),
        [own, pair, peer, across, near],
        "own_place",
        1,
    )
    other = call(join_kernel, bf16((rows_dev + extra, features)), (upper, lower), "other", 1)
    best1 = call(
        near_kernel,
        f32((1, 2 * rows_dev)),
        [after(rows, other), row_labels, best0] + near_pair,
        "beside",
        1,
    )
    other_pair = core(after(other, best1))
    for_far, across_set = call(
        far_kernel,
        (f32((1, rows_dev)), bf16((rows_dev + extra, features))),
        [far, own, pair, across, near] + near_pair + across_pair,
        "far_rows",
        8000000000,
    )
    for_far = call(
        far_other_kernel,
        f32((1, rows_dev)),
        [far, for_far, other, other_pair],
        "far_rows_other",
    )
    from_far = skip_one(for_far)
    mine, for_peer = [
        call(
            functools.partial(rows_kernel, which),
            f32((1, rows_dev)),
            (rows, row_labels, best1, across_set, other, other_pair),
            name,
        )
        for which, name in enumerate(("own_other", "peer_other"))
    ]
    from_peer = middle(for_peer)
    with_far = call(larger_kernel, f32((1, rows_dev)), (mine, from_far), "larger")
    place = lax.axis_index("grp")
    is_inner = (place == inner - 1) | (place == inner)
    return jnp.where(is_inner, jnp.maximum(mine, from_peer), with_far)[0]


def solution(mesh):
    fits = mesh.shape["grp"] == mesh.shape["sub"] == 2 * 2
    return jax.shard_map(
        dense if fits else clustered,
        mesh=mesh,
        in_specs=(P(("rep", "grp", "sub"), None), P(("rep", "grp", "sub"), None)),
        out_specs=P(("rep", "grp", "sub")),
        check_vma=False,
    )
```
